32 devices in a mesh: dp: 4 (over z), table: 8 (over y, x, core).
Axes of the slice: x: 2, y: 2, z: 4, core: 2. Of those that a mesh axis runs over, the one named last changes fastest.
Arguments:
- table_rows: float32 [32768, 64], P(('dp', 'table')), may hold values from -0.9 to 0.9
- hot_rows: float32 [2048, 64], replicated, may hold values from -0.9 to 0.9
- bag_ids: int32 [40, 2048], P(None, 'dp'), may hold values from 0 to 32767, as said below
- bag_weights: float32 [40, 2048], P(None, 'dp'), may hold values from 0.5 to 1.5
- items: float32 [64, 2048], P(None, 'dp'), may hold values from -0.75 to 0.75
- labels: int32 [2048], P('dp'), may hold values 0 or 1
- position_of: int32 [32768], replicated, may hold values from 0 to 32767, each once
- hot_ids: int32 [2048], replicated, may hold values from 0 to 32767, as said below
- table_noise: float32 [32768, 64], P(('dp', 'table')), may hold values from -0.12 to 0.12
- hot_noise: float32 [2048, 64], replicated, may hold values from -0.12 to 0.12
Outputs:
- new_table: float32 [32768, 64], P(('dp', 'table'))
- new_hot: float32 [2048, 64], replicated
The draws below stay inside these ranges and needn't reach their ends.
Inputs may be any that keep to these rules, and one draw needn't show every extreme that they name: `bag_ids`: each draw mixes hot ids and other ids in about equal numbers. `hot_ids`: distinct row ids; ids 0 and 32767 are among them.
All inputs are finite; a program needn't handle non-finite values. No bound on the sum of `labels` on one device may be relied on, other than what follows from the above.
Results may differ from the reference program's by a relative error of at most 0.00007.
Values sent between devices are 32-bit elements; how exact they have to be, the bound alone decides.
A program may use at most 128 MiB of HBM per device.

```python
import jax
import jax.numpy as jnp
from jax import lax

E = 64
BAG = 40
ROWS = 32768
BATCH = 2048
HOT = 2048


def hot_list(key):
    middle = (1 + jax.random.permutation(key, ROWS - 2))[:HOT - 2]
    ends = jnp.array([0, ROWS - 1], dtype=jnp.int32)
    return jnp.concatenate([ends, middle.astype(jnp.int32)]).astype(jnp.int32)


def draw_hot_ids(key, part):
    return hot_list(key)


def draw_bag_ids(key, part):
    hot_set = hot_list(key)
    key = jax.random.fold_in(key, 5)
    key_pick, key_slot, key_cold = jax.random.split(key, 3)
    picked = jax.random.randint(key_pick, (BAG, BATCH), 0, 2)
    slot_pick = jax.random.randint(key_slot, (BAG, BATCH), 0, HOT)
    cold_ids = jax.random.randint(key_cold, (BAG, BATCH), 0, ROWS)
    cold_ids = cold_ids.at[0, 0].set(0).at[BAG - 1, BATCH - 1].set(ROWS - 1)
    picked = picked.at[0, 0].set(0).at[BAG - 1, BATCH - 1].set(0)
    return jnp.where(picked == 1, hot_set[slot_pick], cold_ids).astype(jnp.int32)


def place_ends(entries, rng, low, largest):
    shape = entries.shape
    index_at = [jax.random.randint(jax.random.fold_in(rng, axis), (), 0, shape[axis]) for axis in range(len(shape))]
    entries = entries.at[tuple(index_at)].set(low)
    longest = shape.index(max(shape))
    index_at[longest] = (index_at[longest] + 1) % shape[longest]
    return entries.at[tuple(index_at)].set(largest)


def levels(stream_key, dims, cuts, low, largest):
    def one(axis_at, parts):
        draws = jax.random.uniform(jax.random.fold_in(jax.random.fold_in(stream_key, 6), axis_at), (parts,), jnp.float32, low / len(cuts), largest / len(cuts))
        return jnp.repeat(jnp.exp(draws), dims[axis_at] // parts).reshape((-1,) + (1,) * (len(dims) - axis_at - 1))

    factor_of = one(*cuts[0])
    for cut in cuts[1:]:
        factor_of = factor_of * one(*cut)
    return factor_of


def gaussian(key, extent, width, bound, cuts=(), kind=jnp.bfloat16):
    loudness = levels(key, extent, cuts, -0.22, 0.18) if cuts else 1.0
    result = jax.random.normal(key, extent, jnp.float32) * width * loudness
    return jnp.minimum(jnp.maximum(result, -bound), bound).astype(kind)


def setup_inputs(seed: int = 0) -> dict:
    streams_of = jax.random.split(jax.random.key(seed), 11)
    return {
        "table_rows": gaussian(streams_of[0], (ROWS, E), 0.15, 0.9, ((0, 32),), jnp.float32),
        "hot_rows": gaussian(streams_of[1], (HOT, E), 0.15, 0.9, (), jnp.float32),
        "bag_ids": draw_bag_ids(jax.random.fold_in(streams_of[10], 71), 0),
        "bag_weights": jnp.clip(0.5 + 1.0 * jax.random.uniform(streams_of[3], (BAG, BATCH), jnp.float32) ** levels(streams_of[3], (BAG, BATCH), ((1, 4),), -0.2, 0.2), 0.5, 1.5),
        "items": gaussian(streams_of[4], (E, BATCH), 0.125, 0.75, ((1, 4),), jnp.float32),
        "labels": place_ends((jax.random.randint(streams_of[5], (BATCH,), 0, 2) < 1).astype(jnp.int32), jax.random.fold_in(streams_of[5], 1), 0, 1),
        "position_of": jax.random.permutation(streams_of[6], ROWS).astype(jnp.int32),
        "hot_ids": draw_hot_ids(jax.random.fold_in(streams_of[10], 71), 0),
        "table_noise": gaussian(streams_of[8], (ROWS, E), 0.02, 0.12, ((0, 32),), jnp.float32),
        "hot_noise": gaussian(streams_of[9], (HOT, E), 0.02, 0.12, (), jnp.float32),
    }


LEARN_RATE = 20.0
CLIP_NORM = 1.0

def reference(table_rows, hot_rows, bag_ids, bag_weights, items, labels, position_of, hot_ids, table_noise, hot_noise):
    slot_table = jnp.full((ROWS,), -1, jnp.int32).at[hot_ids].set(jnp.arange(HOT, dtype=jnp.int32))
    hot_slot = slot_table[bag_ids]
    is_hot = hot_slot >= 0
    safe_slot = jnp.maximum(hot_slot, 0)
    stored_at = position_of[bag_ids]
    row_value = jnp.where(is_hot[:, :, None], hot_rows[safe_slot], table_rows[stored_at])
    pooled = jnp.einsum('jb,jbe->eb', bag_weights, row_value)
    scores = lax.optimization_barrier(jnp.sum(pooled * items, axis=0))
    residual_term = jax.nn.sigmoid(scores) - labels.astype(jnp.float32)
    grad_vec = residual_term[None, :] * items
    equal_ids = (bag_ids[:, None, :] == bag_ids[None, :, :]).astype(jnp.float32)
    bag_square = lax.optimization_barrier(jnp.sum(bag_weights[:, None, :] * bag_weights[None, :, :] * equal_ids, axis=(0, 1)))
    norms = jnp.sqrt(bag_square * lax.optimization_barrier(jnp.sum(grad_vec * grad_vec, axis=0)))
    clipped = grad_vec * (CLIP_NORM / jnp.maximum(norms, CLIP_NORM))[None, :]
    contrib = bag_weights[:, :, None] * clipped.T[None, :, :]
    cold_grad = jnp.zeros((ROWS, E), jnp.float32).at[stored_at].add(jnp.where(is_hot[:, :, None], 0.0, contrib))
    hot_grad = jnp.zeros((HOT, E), jnp.float32).at[safe_slot].add(jnp.where(is_hot[:, :, None], contrib, 0.0))
    new_table = table_rows - LEARN_RATE * (cold_grad + CLIP_NORM * table_noise)
    new_hot = hot_rows - LEARN_RATE * (hot_grad + CLIP_NORM * hot_noise)
    return (new_table, new_hot)
```

```python
import functools

import jax
import jax.numpy as jnp
from jax import lax
from jax.experimental import pallas as pl
from jax.experimental.pallas import tpu as pltpu
from jax.sharding import PartitionSpec as P

LEARN_RATE = 20.0
CLIP_NORM = 1.0
LOW = 256
MESH = pl.DeviceIdType.MESH
VMEM = pltpu.VMEM
F32, BF16, I32 = jnp.float32, jnp.bfloat16, jnp.int32
NT = (((1,), (1,)), ((), ()))


def dot(a, b):
    return jnp.dot(a, b, preferred_element_type=F32)


def dot_nt(a, b):
    return lax.dot_general(a, b, NT, preferred_element_type=F32)


def split(x):
    high = x.astype(BF16)
    return high, (x - high.astype(F32)).astype(BF16)


def lookup_kernel(
    data_count, planes, pos_ref, hot_ref, ids_ref, w_ref, items_ref, lab_ref, vals_ref, code_ref,
    slots, table, vs, vr, cs, cr,
):
    d = lax.axis_index("dp")
    t = lax.axis_index("table")
    peers = [lax.rem(d + k, data_count) for k in range(1, data_count)]
    barrier = pltpu.get_barrier_semaphore()
    for peer in peers:
        pl.semaphore_signal(barrier, inc=1, device_id=(peer, t), device_id_type=MESH)
    bag, examples = w_ref.shape
    width = items_ref.shape[0]
    vals_ref[d, 0:bag, :] = w_ref[...]
    vals_ref[d, bag : bag + width, :] = items_ref[...]
    vals_ref[d, bag + width : bag + width + 8, :] = jnp.broadcast_to(
        lab_ref[...].astype(F32), (8, examples)
    )
    pl.semaphore_wait(barrier, data_count - 1)

    def send(ref, send_sem, recv_sem):
        copies = []
        for k, peer in enumerate(peers):
            copies.append(
                pltpu.make_async_remote_copy(
                    src_ref=ref.at[d],
                    dst_ref=ref.at[d],
                    send_sem=send_sem.at[k],
                    recv_sem=recv_sem.at[k],
                    device_id=(peer, t),
                    device_id_type=MESH,
                )
            )
            copies[-1].start()
        return copies

    copies = send(vals_ref, vs, vr)

    high_count = pos_ref.shape[0]
    hot_count = hot_ref.shape[1]
    chunk = min(512, hot_count)
    slots[...] = jnp.zeros_like(slots)

    def add_hot(c, _):
        start = pl.multiple_of(c * chunk, chunk)
        hot = hot_ref[:, pl.ds(start, chunk)]
        number = start + 1 + lax.broadcasted_iota(I32, (1, chunk), 1)
        at_high = lax.broadcasted_iota(I32, (high_count, chunk), 0) == hot // LOW
        at_low = lax.broadcasted_iota(I32, (LOW, chunk), 0) == hot % LOW
        low_hot = jnp.where(at_low, 1.0, 0.0).astype(BF16)
        upper = jnp.where(at_high, (number // 256).astype(F32), 0.0).astype(BF16)
        lower = jnp.where(at_high, (number % 256).astype(F32), 0.0).astype(BF16)
        slots[...] += 256.0 * dot_nt(upper, low_hot) + dot_nt(lower, low_hot)
        return 0

    lax.fori_loop(0, hot_count // chunk, add_hot, 0)
    slot = slots[...].astype(I32)
    code = jnp.where(slot > 0, high_count * LOW - 1 + slot, pos_ref[...])
    for p in range(planes):
        part = lax.shift_right_logical(code, 8 * p) & 255
        table[p * high_count : (p + 1) * high_count, :] = part.astype(F32).astype(BF16)

    def look_up(j, _):
        ids = ids_ref[pl.ds(j, 1), :]
        at_low = lax.broadcasted_iota(I32, (LOW, examples), 0) == ids % LOW
        found = dot(table[...], jnp.where(at_low, 1.0, 0.0).astype(BF16))
        at_high = lax.broadcasted_iota(I32, (high_count, examples), 0) == ids // LOW
        total = jnp.zeros((1, examples), F32)
        for p in range(planes):
            part = found[p * high_count : (p + 1) * high_count]
            total += (256.0**p) * jnp.sum(jnp.where(at_high, part, 0.0), axis=0, keepdims=True)
        code_ref[d, pl.ds(j, 1), :] = total.astype(I32)
        return 0

    lax.fori_loop(0, bag, look_up, 0)
    copies += send(code_ref, cs, cr)
    for copy in copies:
        copy.wait()


def weights_kernel(
    table_count, cold_rows, all_rows, vals_ref, code_ref, ext_ref, high_ref, low_ref, sums_ref, acc, ext
):
    mine = lax.axis_index("dp") * table_count + lax.axis_index("table")
    data_count, bag, examples = code_ref.shape
    width = ext_ref.shape[0]
    rows = ext_ref.shape[1]
    hot_rows = rows - cold_rows
    ext[:width, :], ext[width:, :] = split(ext_ref[...])
    lanes = 128
    blocks = examples // lanes
    earlier = (
        lax.broadcasted_iota(I32, (bag, bag), 1) < lax.broadcasted_iota(I32, (bag, bag), 0)
    )
    earlier = jnp.where(earlier, 1.0, 0.0).astype(BF16)

    for d in range(data_count):
        for c in range(blocks):
            here = pl.ds(c * lanes, lanes)
            code = code_ref[d, :, here]
            cold = code - mine * cold_rows
            hot = code - all_rows - mine * hot_rows
            is_cold = (cold >= 0) & (cold < cold_rows) & (code < all_rows)
            is_hot = (hot >= 0) & (hot < hot_rows)
            owned = is_cold | is_hot
            row = jnp.where(is_cold, cold, hot + cold_rows)
            ones = jnp.where(owned, 1.0, 0.0)
            rank = dot(earlier, ones.astype(BF16)).astype(I32)
            rank = jnp.where(owned, rank, -1)
            weight = vals_ref[d, 0:bag, here]
            count = jnp.max(jnp.sum(ones, axis=0, keepdims=True)).astype(I32)
            acc[...] = jnp.zeros_like(acc)
            numbers = lax.broadcasted_iota(I32, (rows, lanes), 0)

            def place(i, _):
                total = acc[...]
                for u in range(2):
                    this = rank == 2 * i + u
                    at = jnp.sum(jnp.where(this, row + 1, 0), axis=0, keepdims=True) - 1
                    w = jnp.sum(jnp.where(this, weight, 0.0), axis=0, keepdims=True)
                    total += jnp.where(numbers == at, w, 0.0)
                acc[...] = total
                return 0

            lax.fori_loop(0, (count + 1) // 2, place, 0)
            total = acc[...]
            high, low = split(total)
            out = pl.ds(d * examples + c * lanes, lanes)
            high_ref[:, out] = high
            low_ref[:, out] = low
            first = dot(ext[...], high)
            pooled = first[:width] + first[width:] + dot(ext[:width, :], low)
            items = vals_ref[d, bag : bag + width, here]
            sums_ref[pl.ds(d, 1), here] = jnp.sum(pooled * items, axis=0, keepdims=True)
            sums_ref[pl.ds(data_count + d, 1), here] = jnp.sum(
                total * total, axis=0, keepdims=True
            )


def update_kernel(
    data_count, table_count, bag, sums_ref, vals_ref, high_ref, low_ref, table_ref, noise_ref,
    hot_ref, hot_noise_ref, new_table_ref, new_hot_ref,
    over_table, over_data, hot_all, clip_all, as_, ar, bs, br, hs, hr, gs, gr,
):
    d = lax.axis_index("dp")
    t = lax.axis_index("table")
    data_peers = [(lax.rem(d + k, data_count), t) for k in range(1, data_count)]
    table_peers = [(d, lax.rem(t + k, table_count)) for k in range(1, table_count)]
    barrier = pltpu.get_barrier_semaphore()
    for peer in data_peers + table_peers:
        pl.semaphore_signal(barrier, inc=1, device_id=peer, device_id_type=MESH)
    pl.semaphore_wait(barrier, data_count + table_count - 2)

    def exchange(ref, at, peers, send_sem, recv_sem):
        copies = []
        for k, peer in enumerate(peers):
            copies.append(
                pltpu.make_async_remote_copy(
                    src_ref=ref.at[at],
                    dst_ref=ref.at[at],
                    send_sem=send_sem.at[k],
                    recv_sem=recv_sem.at[k],
                    device_id=peer,
                    device_id_type=MESH,
                )
            )
            copies[-1].start()
        return copies

    over_table[t] = sums_ref[...]
    for copy in exchange(over_table, t, table_peers, as_, ar):
        copy.wait()
    total = over_table[0]
    for k in range(1, table_count):
        total += over_table[k]
    over_data[d] = total
    for copy in exchange(over_data, d, data_peers, bs, br):
        copy.wait()
    total = over_data[0]
    for k in range(1, data_count):
        total += over_data[k]

    width = table_ref.shape[1]
    examples = sums_ref.shape[1]
    cold_rows = table_ref.shape[0]
    rows = high_ref.shape[0]
    for k in range(data_count):
        items = vals_ref[k, bag : bag + width, :]
        labels = vals_ref[k, bag + width : bag + width + 1, :]
        residual = jax.nn.sigmoid(total[k : k + 1]) - labels
        grad = residual * items
        square = jnp.sum(grad * grad, axis=0, keepdims=True)
        norms = jnp.sqrt(total[data_count + k : data_count + k + 1] * square)
        high, low = split(grad * (CLIP_NORM / jnp.maximum(norms, CLIP_NORM)))
        here = pl.ds(k * examples, examples)
        clip_all[:width, here] = high
        clip_all[width:, here] = low

    def gradient(start, size):
        both = dot_nt(high_ref[pl.ds(start, size), :], clip_all[...])
        rest = dot_nt(low_ref[pl.ds(start, size), :], clip_all[:width, :])
        return both[:, :width] + both[:, width:] + rest

    hot_own = gradient(cold_rows, rows - cold_rows)
    mine = d * table_count + t
    hot_all[mine] = hot_ref[...] - LEARN_RATE * (hot_own + CLIP_NORM * hot_noise_ref[...])
    first = exchange(hot_all, mine, data_peers, hs, hr)

    def update(start, size):
        here = pl.ds(start, size)
        new_table_ref[here, :] = table_ref[here, :] - LEARN_RATE * (
            gradient(start, size) + CLIP_NORM * noise_ref[here, :]
        )

    step = cold_rows // 4
    update(0, step)
    for copy in first:
        copy.wait()
    second = []
    for k in range(data_count):
        at = lax.rem(d + k, data_count) * table_count + t
        second += exchange(hot_all, at, table_peers, gs.at[k], gr.at[k])
    for i in range(1, 4):
        update(i * step, step)
    for copy in second:
        copy.wait()
    new_hot_ref[...] = hot_all[...]


def per_device(
    table_rows,
    hot_rows,
    bag_ids,
    bag_weights,
    items,
    labels,
    position_of,
    hot_ids,
    table_noise,
    hot_noise,
):
    cold_rows, width = table_rows.shape
    all_rows = position_of.shape[0]
    hot_count = hot_ids.shape[0]
    bag, examples = bag_ids.shape
    table_count = lax.axis_size("table")
    data_count = lax.axis_size("dp")
    devices = table_count * data_count
    mine = lax.axis_index("dp") * table_count + lax.axis_index("table")
    hot_own = hot_count // devices
    rows = cold_rows + hot_own
    high_count = all_rows // LOW
    planes = 1
    while 256**planes < all_rows + hot_count:
        planes += 1
    value_rows = bag + width + 8
    limit = 56 * 1024 * 1024
    vmem = pl.BlockSpec(memory_space=VMEM)
    dma = pltpu.SemaphoreType.DMA

    vals, code = pl.pallas_call(
        functools.partial(lookup_kernel, data_count, planes),
        out_shape=(
            jax.ShapeDtypeStruct((data_count, value_rows, examples), F32),
            jax.ShapeDtypeStruct((data_count, bag, examples), I32),
        ),
        in_specs=[vmem] * 6,
        out_specs=(vmem, vmem),
        scratch_shapes=[
            VMEM((high_count, LOW), F32),
            VMEM((planes * high_count, LOW), BF16),
        ]
        + [dma((data_count - 1,))] * 4,
        compiler_params=pltpu.CompilerParams(
            collective_id=0, has_side_effects=True, vmem_limit_bytes=limit
        ),
    )(
        position_of.reshape(high_count, LOW),
        hot_ids.reshape(1, hot_count),
        bag_ids,
        bag_weights,
        items,
        labels.reshape(1, examples),
    )

    hot_mine = lax.dynamic_slice_in_dim(hot_rows, mine * hot_own, hot_own, 0)
    hot_noise_mine = lax.dynamic_slice_in_dim(hot_noise, mine * hot_own, hot_own, 0)
    ext = jnp.concatenate([table_rows, hot_mine], axis=0).T

    high, low, sums = pl.pallas_call(
        functools.partial(weights_kernel, table_count, cold_rows, all_rows),
        out_shape=(
            jax.ShapeDtypeStruct((rows, data_count * examples), BF16),
            jax.ShapeDtypeStruct((rows, data_count * examples), BF16),
            jax.ShapeDtypeStruct((2 * data_count, examples), F32),
        ),
        in_specs=[vmem] * 3,
        out_specs=(vmem, vmem, vmem),
        scratch_shapes=[VMEM((rows, 128), F32), VMEM((2 * width, rows), BF16)],
        compiler_params=pltpu.CompilerParams(vmem_limit_bytes=limit),
    )(vals, code, ext)

    new_table, new_hot = pl.pallas_call(
        functools.partial(update_kernel, data_count, table_count, bag),
        out_shape=(
            jax.ShapeDtypeStruct((cold_rows, width), F32),
            jax.ShapeDtypeStruct((devices, hot_own, width), F32),
        ),
        in_specs=[vmem] * 8,
        out_specs=(vmem, vmem),
        scratch_shapes=[
            VMEM((table_count, 2 * data_count, examples), F32),
            VMEM((data_count, 2 * data_count, examples), F32),
            VMEM((devices, hot_own, width), F32),
            VMEM((2 * width, data_count * examples), BF16),
            dma((table_count - 1,)),
            dma((table_count - 1,)),
            dma((data_count - 1,)),
            dma((data_count - 1,)),
            dma((data_count - 1,)),
            dma((data_count - 1,)),
            dma((data_count, table_count - 1)),
            dma((data_count, table_count - 1)),
        ],
        compiler_params=pltpu.CompilerParams(
            collective_id=1, has_side_effects=True, vmem_limit_bytes=limit
        ),
    )(sums, vals, high, low, table_rows, table_noise, hot_mine, hot_noise_mine)
    return (new_table, new_hot.reshape(hot_count, width))


def solution(mesh):
    return jax.shard_map(
        per_device,
        mesh=mesh,
        in_specs=(
            P(("dp", "table"), None),
            P(),
            P(None, "dp"),
            P(None, "dp"),
            P(None, "dp"),
            P("dp"),
            P(),
            P(),
            P(("dp", "table"), None),
            P(),
        ),
        out_specs=(P(("dp", "table"), None), P()),
        check_vma=False,
    )
```

```python
import functools

import jax
import jax.numpy as jnp
from jax import lax
from jax.experimental import pallas as pl
from jax.experimental.pallas import tpu as pltpu
from jax.sharding import PartitionSpec as P

LEARN_RATE = 20.0
CLIP_NORM = 1.0
LOW = 128
MESH = pl.DeviceIdType.MESH
VMEM = pltpu.VMEM
F32, BF16, I32 = jnp.float32, jnp.bfloat16, jnp.int32
NT = (((1,), (1,)), ((), ()))


def dot(a, b):
    return jnp.dot(a, b, preferred_element_type=F32)


def dot_nt(a, b):
    return lax.dot_general(a, b, NT, preferred_element_type=F32)


def split(x):
    high = x.astype(BF16)
    return high, (x - high.astype(F32)).astype(BF16)


def remote(ref, at, peer, send_sem, recv_sem):
    copy = pltpu.make_async_remote_copy(
        src_ref=ref.at[at],
        dst_ref=ref.at[at],
        send_sem=send_sem,
        recv_sem=recv_sem,
        device_id=peer,
        device_id_type=MESH,
    )
    copy.start()
    return copy


class Spread:
    def __init__(self, ref, sizes, own, sems):
        self.ref, self.own, self.sems = ref, own, sems
        self.data_count, self.table_count = sizes
        self.d, self.t = lax.axis_index("dp"), lax.axis_index("table")
        self.alike = [
            lax.rem(self.t + 2 * i, self.table_count) for i in range(1, self.table_count // 2)
        ]
        self.partner = self.t + 1 - 2 * lax.rem(self.t, 2)
        self.first, self.second, self.third = [], [], []

    def group(self, k):
        return lax.rem(self.d + self.data_count - k, self.data_count)

    def over_data(self):
        for k in range(1, self.data_count):
            peer = (lax.rem(self.d + k, self.data_count), self.t)
            sems = self.sems[0].at[k], self.sems[1].at[k]
            self.first.append(remote(self.ref, (self.t, self.d), peer, *sems))

    def over_table(self):
        for k in range(0 if self.own else 1, self.data_count):
            if k:
                self.first[k - 1].wait_recv()
            at = (self.t, self.group(k))
            for i, peer in enumerate(self.alike):
                sems = self.sems[2].at[k, i], self.sems[3].at[k, i]
                self.second.append((k, i, remote(self.ref, at, (self.d, peer), *sems)))
            self.to_partner(k, 0)

    def to_partner(self, k, i):
        at = (lax.rem(self.t + self.table_count - 2 * i, self.table_count), self.group(k))
        sems = self.sems[4].at[k, i], self.sems[5].at[k, i]
        self.third.append(remote(self.ref, at, (self.d, self.partner), *sems))

    def over_pair(self):
        for k, i, copy in self.second:
            copy.wait_recv()
            self.to_partner(k, i + 1)

    def finish(self):
        for copy in self.third:
            copy.wait_recv()
        for copy in self.first + [copy for _, _, copy in self.second] + self.third:
            copy.wait_send()


def tile_of(ref, d, tile, lanes=slice(None)):
    per = ref.shape[2] // 8
    return ref[tile // per, d, tile % per * 8 : tile % per * 8 + 8, lanes]


def rows_of(ref, d, start, stop, lanes=slice(None)):
    return jnp.concatenate(
        [tile_of(ref, d, tile, lanes) for tile in range(start // 8, stop // 8)], axis=0
    )


def lookup_kernel(
    data_count, table_count, planes, pos_ref, hot_ref, ids_ref, w_ref, items_ref, lab_ref,
    vals_ref, code_ref, slots, table, *sems,
):
    d = lax.axis_index("dp")
    t = lax.axis_index("table")
    sizes = (data_count, table_count)
    vals = Spread(vals_ref, sizes, False, sems[:6])
    codes = Spread(code_ref, sizes, True, sems[6:])
    barrier = pltpu.get_barrier_semaphore()
    peers = [(lax.rem(d + k, data_count), t) for k in range(1, data_count)]
    peers += [(d, peer) for peer in vals.alike + [vals.partner]]
    for peer in peers:
        pl.semaphore_signal(barrier, inc=1, device_id=peer, device_id_type=MESH)
    bag, examples = w_ref.shape
    width = items_ref.shape[0]
    per = vals_ref.shape[2] // 8
    label = jnp.broadcast_to(lab_ref[...].astype(F32), (8, examples))
    for tile in range(table_count * per):
        start = tile * 8
        if start < bag:
            part = w_ref[start : start + 8, :]
        elif start < bag + width:
            part = items_ref[start - bag : start - bag + 8, :]
        else:
            part = label
        vals_ref[tile // per, d, tile % per * 8 : tile % per * 8 + 8, :] = part
    pl.semaphore_wait(barrier, len(peers))
    vals.over_data()

    high_count = pos_ref.shape[0]
    hot_count = hot_ref.shape[1]
    chunk = min(512, hot_count)
    slots[...] = jnp.zeros_like(slots)

    def add_hot(c, _):
        start = pl.multiple_of(c * chunk, chunk)
        hot = hot_ref[:, pl.ds(start, chunk)]
        number = start + 1 + lax.broadcasted_iota(I32, (1, chunk), 1)
        at_high = lax.broadcasted_iota(I32, (high_count, chunk), 0) == hot // LOW
        at_low = lax.broadcasted_iota(I32, (LOW, chunk), 0) == hot % LOW
        low_hot = jnp.where(at_low, 1.0, 0.0).astype(BF16)
        upper = jnp.where(at_high, (number // 256).astype(F32), 0.0).astype(BF16)
        lower = jnp.where(at_high, (number % 256).astype(F32), 0.0).astype(BF16)
        slots[...] += 256.0 * dot_nt(upper, low_hot) + dot_nt(lower, low_hot)
        return 0

    lax.fori_loop(0, hot_count // chunk, add_hot, 0)
    slot = slots[...].astype(I32)
    code = jnp.where(slot > 0, high_count * LOW - 1 + slot, pos_ref[...])
    for p in range(planes):
        part = lax.shift_right_logical(code, 8 * p) & 255
        table[p * high_count : (p + 1) * high_count, :] = part.astype(F32).astype(BF16)
    vals.over_table()

    mine = pl.multiple_of(jnp.minimum(t, bag // 8 - 1) * 8, 8)

    def look_up(j, _):
        ids = ids_ref[pl.ds(mine + j, 1), :]
        at_low = lax.broadcasted_iota(I32, (LOW, examples), 0) == ids % LOW
        found = dot(table[...], jnp.where(at_low, 1.0, 0.0).astype(BF16))
        at_high = lax.broadcasted_iota(I32, (high_count, examples), 0) == ids // LOW
        total = jnp.zeros((1, examples), F32)
        for p in range(planes):
            part = found[p * high_count : (p + 1) * high_count]
            total += (256.0**p) * jnp.sum(jnp.where(at_high, part, 0.0), axis=0, keepdims=True)
        code_ref[t, d, pl.ds(j, 1), :] = total.astype(I32)
        return 0

    lax.fori_loop(0, 8, look_up, 0)
    codes.over_data()
    vals.over_pair()
    codes.over_table()
    codes.over_pair()
    vals.finish()
    codes.finish()


def weights_kernel(
    sizes, bag, all_rows, vals_ref, code_ref, cold_ref, hot_ref, high_ref, low_ref, sums_ref,
    acc, ext, shares,
):
    data_count, table_count = sizes
    mine = lax.axis_index("dp") * table_count + lax.axis_index("table")
    d = pl.program_id(0)
    examples = code_ref.shape[3]
    width, cold_rows = cold_ref.shape
    hot_rows = hot_ref.shape[1]
    rows = cold_rows + hot_rows
    lanes = 128

    @pl.when(d == 0)
    def _():
        for start, part in ((0, cold_ref[...].T), (cold_rows, hot_ref[...].T)):
            high, low = split(part)
            here = pl.ds(start, part.shape[0])
            ext[here, :width] = high
            ext[here, width : 2 * width] = low
            ext[here, 2 * width :] = high

    earlier = (
        lax.broadcasted_iota(I32, (bag, bag), 1) < lax.broadcasted_iota(I32, (bag, bag), 0)
    )
    earlier = jnp.where(earlier, 1.0, 0.0).astype(BF16)
    high, low = split(rows_of(vals_ref, d, bag, bag + width))
    shares[...] = dot(ext[...], jnp.concatenate([high, high, low], axis=0))

    scores, squares = [], []
    for c in range(examples // lanes):
        here = pl.ds(c * lanes, lanes)
        code = rows_of(code_ref, d, 0, bag, here)
        cold = code - mine * cold_rows
        hot = code - all_rows - mine * hot_rows
        is_cold = (cold >= 0) & (cold < cold_rows) & (code < all_rows)
        is_hot = (hot >= 0) & (hot < hot_rows)
        owned = is_cold | is_hot
        row = jnp.where(is_cold, cold, hot + cold_rows)
        ones = jnp.where(owned, 1.0, 0.0)
        rank = dot(earlier, ones.astype(BF16)).astype(I32)
        rank = jnp.where(owned, rank, -1)
        weight = rows_of(vals_ref, d, 0, bag, here)
        count = jnp.max(jnp.sum(ones, axis=0, keepdims=True)).astype(I32)
        numbers = lax.broadcasted_iota(I32, (rows, lanes), 0)

        def pair(i):
            total = 0.0
            for u in range(2):
                this = rank == 2 * i + u
                at = jnp.sum(jnp.where(this, row + 1, 0), axis=0, keepdims=True) - 1
                w = jnp.sum(jnp.where(this, weight, 0.0), axis=0, keepdims=True)
                total = total + jnp.where(numbers == at, w, 0.0)
            return total

        acc[...] = pair(0)

        def place(i, _):
            acc[...] += pair(i)
            return 0

        lax.fori_loop(1, (count + 1) // 2, place, 0)
        total = acc[...]
        high, low = split(total)
        high_ref[:, here] = high
        low_ref[:, here] = low
        scores.append(jnp.sum(total * shares[:, here], axis=0, keepdims=True))
        squares.append(jnp.sum(total * total, axis=0, keepdims=True))
    sums_ref[pl.ds(d, 1), :] = jnp.concatenate(scores, axis=1)
    sums_ref[pl.ds(data_count + d, 1), :] = jnp.concatenate(squares, axis=1)


def update_kernel(
    data_count, table_count, bag, sums_ref, vals_ref, high_hbm, low_hbm, table_ref, noise_ref,
    hot_ref, hot_noise_ref, new_table_ref, new_hot_ref, high_ref, low_ref,
    over_table, over_data, hot_all, clip_all, load, as_, ar, bs, br, hs, hr, gs, gr,
):
    d = lax.axis_index("dp")
    t = lax.axis_index("table")
    loads = [
        pltpu.make_async_copy(high_hbm, high_ref, load.at[0]),
        pltpu.make_async_copy(low_hbm, low_ref, load.at[1]),
    ]
    data_peers = [(lax.rem(d + k, data_count), t) for k in range(1, data_count)]
    table_peers = [(d, lax.rem(t + k, table_count)) for k in range(1, table_count)]
    barrier = pltpu.get_barrier_semaphore()
    for peer in data_peers + table_peers:
        pl.semaphore_signal(barrier, inc=1, device_id=peer, device_id_type=MESH)
    for copy in loads:
        copy.start()
    pl.semaphore_wait(barrier, data_count + table_count - 2)

    def exchange(ref, at, peers, send_sem, recv_sem):
        return [
            remote(ref, at, peer, send_sem.at[k], recv_sem.at[k]) for k, peer in enumerate(peers)
        ]

    over_table[t] = sums_ref[...]
    for copy in exchange(over_table, t, table_peers, as_, ar):
        copy.wait()
    total = over_table[0]
    for k in range(1, table_count):
        total += over_table[k]
    over_data[d] = total
    for copy in exchange(over_data, d, data_peers, bs, br):
        copy.wait()
    total = over_data[0]
    for k in range(1, data_count):
        total += over_data[k]

    width, cold_rows = table_ref.shape
    examples = sums_ref.shape[1]
    rows = high_ref.shape[0]
    hot_rows = rows - cold_rows
    for k in range(data_count):
        items = rows_of(vals_ref, k, bag, bag + width)
        labels = tile_of(vals_ref, k, (bag + width) // 8)[0:1]
        residual = jax.nn.sigmoid(total[k : k + 1]) - labels
        grad = residual * items
        square = jnp.sum(grad * grad, axis=0, keepdims=True)
        norms = jnp.sqrt(total[data_count + k : data_count + k + 1] * square)
        high, low = split(grad * (CLIP_NORM / jnp.maximum(norms, CLIP_NORM)))
        here = pl.ds(k * examples, examples)
        clip_all[:width, here] = high
        clip_all[width:, here] = low

    for copy in loads:
        copy.wait()

    def gradient(start, size):
        both = dot_nt(clip_all[...], high_ref[pl.ds(start, size), :])
        rest = dot_nt(clip_all[:width, :], low_ref[pl.ds(start, size), :])
        return both[:width] + both[width:] + rest

    hot_own = gradient(cold_rows, hot_rows)
    mine = d * table_count + t
    half = width // 2
    hot_all[mine] = jnp.concatenate([hot_own[:half], hot_own[half:]], axis=1)
    first = exchange(hot_all, mine, data_peers, hs, hr)

    def update(start, size):
        here = pl.ds(start, size)
        new_table_ref[:, here] = table_ref[:, here] - LEARN_RATE * (
            gradient(start, size) + CLIP_NORM * noise_ref[:, here]
        )

    step = cold_rows // 4
    update(0, step)
    for copy in first:
        copy.wait()
    second = []
    for k in range(data_count):
        at = lax.rem(d + k, data_count) * table_count + t
        second += exchange(hot_all, at, table_peers, gs.at[k], gr.at[k])
    for i in range(1, 4):
        update(i * step, step)
    for copy in second:
        copy.wait()
    for pair in range(data_count * table_count // 2):
        here = pl.ds(pair * 2 * hot_rows, 2 * hot_rows)
        left, right = hot_all[2 * pair], hot_all[2 * pair + 1]
        upper = jnp.concatenate([left[:, :hot_rows], right[:, :hot_rows]], axis=1)
        lower = jnp.concatenate([left[:, hot_rows:], right[:, hot_rows:]], axis=1)
        new_hot_ref[:, here] = hot_ref[:, here] - LEARN_RATE * (
            jnp.concatenate([upper, lower], axis=0) + CLIP_NORM * hot_noise_ref[:, here]
        )


def per_device(
    table_rows,
    hot_rows,
    bag_ids,
    bag_weights,
    items,
    labels,
    position_of,
    hot_ids,
    table_noise,
    hot_noise,
):
    cold_rows, width = table_rows.shape
    all_rows = position_of.shape[0]
    hot_count = hot_ids.shape[0]
    bag, examples = bag_ids.shape
    table_count = lax.axis_size("table")
    data_count = lax.axis_size("dp")
    devices = table_count * data_count
    mine = lax.axis_index("dp") * table_count + lax.axis_index("table")
    hot_own = hot_count // devices
    rows = cold_rows + hot_own
    high_count = all_rows // LOW
    planes = 1
    while 256**planes < all_rows + hot_count:
        planes += 1
    tiles = (bag + width) // 8 + 1
    chunk_rows = 8 * (-(-tiles // table_count))
    assert bag // 8 <= table_count and 2 * hot_own == 128 and width == hot_own
    limit = 56 * 1024 * 1024
    vmem = pl.BlockSpec(memory_space=VMEM)
    dma = pltpu.SemaphoreType.DMA
    half = table_count // 2
    spread = [dma((data_count,))] * 2 + [dma((data_count, half))] * 4

    vals, code = pl.pallas_call(
        functools.partial(lookup_kernel, data_count, table_count, planes),
        out_shape=(
            jax.ShapeDtypeStruct((table_count, data_count, chunk_rows, examples), F32),
            jax.ShapeDtypeStruct((table_count, data_count, 8, examples), I32),
        ),
        in_specs=[vmem] * 6,
        out_specs=(vmem, vmem),
        scratch_shapes=[
            VMEM((high_count, LOW), F32),
            VMEM((planes * high_count, LOW), BF16),
        ]
        + spread
        + spread,
        compiler_params=pltpu.CompilerParams(
            collective_id=0, has_side_effects=True, vmem_limit_bytes=limit
        ),
    )(
        position_of.reshape(high_count, LOW),
        hot_ids.reshape(1, hot_count),
        bag_ids,
        bag_weights,
        items,
        labels.reshape(1, examples),
    )

    hot_mine = lax.dynamic_slice_in_dim(hot_rows, mine * hot_own, hot_own, 0)

    def whole(*shape):
        return pl.BlockSpec(shape, lambda d: (0,) * len(shape))

    high, low, sums = pl.pallas_call(
        functools.partial(weights_kernel, (data_count, table_count), bag, all_rows),
        grid=(data_count,),
        out_shape=(
            jax.ShapeDtypeStruct((rows, data_count * examples), BF16),
            jax.ShapeDtypeStruct((rows, data_count * examples), BF16),
            jax.ShapeDtypeStruct((2 * data_count, examples), F32),
        ),
        in_specs=[
            whole(*vals.shape),
            whole(*code.shape),
            whole(width, cold_rows),
            whole(width, hot_own),
        ],
        out_specs=(
            pl.BlockSpec((rows, examples), lambda d: (0, d)),
            pl.BlockSpec((rows, examples), lambda d: (0, d)),
            whole(2 * data_count, examples),
        ),
        scratch_shapes=[
            VMEM((rows, 128), F32),
            VMEM((rows, 3 * width), BF16),
            VMEM((rows, examples), F32),
        ],
        compiler_params=pltpu.CompilerParams(vmem_limit_bytes=limit),
    )(vals, code, table_rows.T, hot_mine.T)

    new_table, new_hot = pl.pallas_call(
        functools.partial(update_kernel, data_count, table_count, bag),
        out_shape=(
            jax.ShapeDtypeStruct((width, cold_rows), F32),
            jax.ShapeDtypeStruct((width, hot_count), F32),
        ),
        in_specs=[vmem] * 2 + [pl.BlockSpec(memory_space=pl.ANY)] * 2 + [vmem] * 4,
        out_specs=(vmem, vmem),
        scratch_shapes=[
            VMEM((rows, data_count * examples), BF16),
            VMEM((rows, data_count * examples), BF16),
            VMEM((table_count, 2 * data_count, examples), F32),
            VMEM((data_count, 2 * data_count, examples), F32),
            VMEM((devices, width // 2, 2 * hot_own), F32),
            VMEM((2 * width, data_count * examples), BF16),
            dma((2,)),
            dma((table_count - 1,)),
            dma((table_count - 1,)),
            dma((data_count - 1,)),
            dma((data_count - 1,)),
            dma((data_count - 1,)),
            dma((data_count - 1,)),
            dma((data_count, table_count - 1)),
            dma((data_count, table_count - 1)),
        ],
        compiler_params=pltpu.CompilerParams(
            collective_id=1, has_side_effects=True, vmem_limit_bytes=limit
        ),
    )(sums, vals, high, low, table_rows.T, table_noise.T, hot_rows.T, hot_noise.T)
    return (new_table.T, new_hot.T)


def solution(mesh):
    return jax.shard_map(
        per_device,
        mesh=mesh,
        in_specs=(
            P(("dp", "table"), None),
            P(),
            P(None, "dp"),
            P(None, "dp"),
            P(None, "dp"),
            P("dp"),
            P(),
            P(),
            P(("dp", "table"), None),
            P(),
        ),
        out_specs=(P(("dp", "table"), None), P()),
        check_vma=False,
    )
```

```python
import functools

import jax
import jax.numpy as jnp
from jax import lax
from jax.experimental import pallas as pl
from jax.experimental.pallas import tpu as pltpu
from jax.sharding import PartitionSpec as P

LEARN_RATE = 20.0
CLIP_NORM = 1.0
LOW = 128
MESH = pl.DeviceIdType.MESH
VMEM = pltpu.VMEM
F32, BF16, I32 = jnp.float32, jnp.bfloat16, jnp.int32
NT = (((1,), (1,)), ((), ()))


def dot(a, b):
    return jnp.dot(a, b, preferred_element_type=F32)


def dot_nt(a, b):
    return lax.dot_general(a, b, NT, preferred_element_type=F32)


def split(x):
    high = x.astype(BF16)
    return high, (x - high.astype(F32)).astype(BF16)


def remote(ref, at, peer, send_sem, recv_sem):
    copy = pltpu.make_async_remote_copy(
        src_ref=ref.at[at],
        dst_ref=ref.at[at],
        send_sem=send_sem,
        recv_sem=recv_sem,
        device_id=peer,
        device_id_type=MESH,
    )
    copy.start()
    return copy


class Spread:
    def __init__(self, ref, sizes, own, sems):
        self.ref, self.own, self.sems = ref, own, sems
        self.data_count, self.table_count = sizes
        self.d, self.t = lax.axis_index("dp"), lax.axis_index("table")
        self.alike = [
            lax.rem(self.t + 2 * i, self.table_count) for i in range(1, self.table_count // 2)
        ]
        self.partner = self.t + 1 - 2 * lax.rem(self.t, 2)
        self.first, self.second, self.third = [], [], []

    def group(self, k):
        return lax.rem(self.d + self.data_count - k, self.data_count)

    def over_data(self):
        for k in range(1, self.data_count):
            peer = (lax.rem(self.d + k, self.data_count), self.t)
            sems = self.sems[0].at[k], self.sems[1].at[k]
            self.first.append(remote(self.ref, (self.t, self.d), peer, *sems))

    def over_table(self):
        for k in range(0 if self.own else 1, self.data_count):
            if k:
                self.first[k - 1].wait_recv()
            at = (self.t, self.group(k))
            for i, peer in enumerate(self.alike):
                sems = self.sems[2].at[k, i], self.sems[3].at[k, i]
                self.second.append((k, i, remote(self.ref, at, (self.d, peer), *sems)))
            self.to_partner(k, 0)

    def to_partner(self, k, i):
        at = (lax.rem(self.t + self.table_count - 2 * i, self.table_count), self.group(k))
        sems = self.sems[4].at[k, i], self.sems[5].at[k, i]
        self.third.append(remote(self.ref, at, (self.d, self.partner), *sems))

    def over_pair(self):
        for k, i, copy in self.second:
            copy.wait_recv()
            self.to_partner(k, i + 1)

    def finish(self):
        for copy in self.third:
            copy.wait_recv()
        for copy in self.first + [copy for _, _, copy in self.second] + self.third:
            copy.wait_send()


def tile_of(ref, d, tile, lanes=slice(None)):
    per = ref.shape[2] // 8
    return ref[tile // per, d, tile % per * 8 : tile % per * 8 + 8, lanes]


def rows_of(ref, d, start, stop, lanes=slice(None)):
    return jnp.concatenate(
        [tile_of(ref, d, tile, lanes) for tile in range(start // 8, stop // 8)], axis=0
    )


def lookup_kernel(
    data_count, table_count, planes, pos_ref, hot_ref, ids_ref, w_ref, items_ref, lab_ref,
    vals_ref, code_ref, slots, table, *sems,
):
    d = lax.axis_index("dp")
    t = lax.axis_index("table")
    sizes = (data_count, table_count)
    vals = Spread(vals_ref, sizes, False, sems[:6])
    codes = Spread(code_ref, sizes, True, sems[6:])
    barrier = pltpu.get_barrier_semaphore()
    peers = [(lax.rem(d + k, data_count), t) for k in range(1, data_count)]
    peers += [(d, peer) for peer in vals.alike + [vals.partner]]
    for peer in peers:
        pl.semaphore_signal(barrier, inc=1, device_id=peer, device_id_type=MESH)
    bag, examples = w_ref.shape
    width = items_ref.shape[0]
    per = vals_ref.shape[2] // 8
    label = jnp.broadcast_to(lab_ref[...].astype(F32), (8, examples))
    for tile in range(table_count * per):
        start = tile * 8
        if start < bag:
            part = w_ref[start : start + 8, :]
        elif start < bag + width:
            part = items_ref[start - bag : start - bag + 8, :]
        else:
            part = label
        vals_ref[tile // per, d, tile % per * 8 : tile % per * 8 + 8, :] = part
    pl.semaphore_wait(barrier, len(peers))
    vals.over_data()

    high_count = pos_ref.shape[0]
    hot_count = hot_ref.shape[1]
    chunk = min(512, hot_count)
    slots[...] = jnp.zeros_like(slots)

    def add_hot(c, _):
        start = pl.multiple_of(c * chunk, chunk)
        hot = hot_ref[:, pl.ds(start, chunk)]
        number = start + 1 + lax.broadcasted_iota(I32, (1, chunk), 1)
        at_high = lax.broadcasted_iota(I32, (high_count, chunk), 0) == hot // LOW
        at_low = lax.broadcasted_iota(I32, (LOW, chunk), 0) == hot % LOW
        low_hot = jnp.where(at_low, 1.0, 0.0).astype(BF16)
        upper = jnp.where(at_high, (number // 256).astype(F32), 0.0).astype(BF16)
        lower = jnp.where(at_high, (number % 256).astype(F32), 0.0).astype(BF16)
        slots[...] += 256.0 * dot_nt(upper, low_hot) + dot_nt(lower, low_hot)
        return 0

    lax.fori_loop(0, hot_count // chunk, add_hot, 0)
    slot = slots[...].astype(I32)
    code = jnp.where(slot > 0, high_count * LOW - 1 + slot, pos_ref[...])
    for p in range(planes):
        part = lax.shift_right_logical(code, 8 * p) & 255
        table[p * high_count : (p + 1) * high_count, :] = part.astype(F32).astype(BF16)
    vals.over_table()

    mine = pl.multiple_of(jnp.minimum(t, bag // 8 - 1) * 8, 8)

    def look_up(j, _):
        ids = ids_ref[pl.ds(mine + j, 1), :]
        at_low = lax.broadcasted_iota(I32, (LOW, examples), 0) == ids % LOW
        found = dot(table[...], jnp.where(at_low, 1.0, 0.0).astype(BF16))
        at_high = lax.broadcasted_iota(I32, (high_count, examples), 0) == ids // LOW
        total = jnp.zeros((1, examples), F32)
        for p in range(planes):
            part = found[p * high_count : (p + 1) * high_count]
            total += (256.0**p) * jnp.sum(jnp.where(at_high, part, 0.0), axis=0, keepdims=True)
        code_ref[t, d, pl.ds(j, 1), :] = total.astype(I32)
        return 0

    lax.fori_loop(0, 8, look_up, 0)
    codes.over_data()
    codes.over_table()
    vals.over_pair()
    codes.over_pair()
    vals.finish()
    codes.finish()


def weights_kernel(
    sizes, bag, all_rows, vals_ref, code_ref, cold_ref, hot_ref, high_ref, low_ref, sums_ref,
    acc, ext, shares, at_rank, w_rank,
):
    data_count, table_count = sizes
    mine = lax.axis_index("dp") * table_count + lax.axis_index("table")
    d = pl.program_id(0)
    examples = code_ref.shape[3]
    width, cold_rows = cold_ref.shape
    hot_rows = hot_ref.shape[1]
    rows = cold_rows + hot_rows
    lanes = 128

    @pl.when(d == 0)
    def _():
        for start, part in ((0, cold_ref[...].T), (cold_rows, hot_ref[...].T)):
            high, low = split(part)
            here = pl.ds(start, part.shape[0])
            ext[here, :width] = high
            ext[here, width : 2 * width] = low
            ext[here, 2 * width :] = high

    earlier = (
        lax.broadcasted_iota(I32, (bag, bag), 1) < lax.broadcasted_iota(I32, (bag, bag), 0)
    )
    earlier = jnp.where(earlier, 1.0, 0.0).astype(BF16)
    high, low = split(rows_of(vals_ref, d, bag, bag + width))
    shares[...] = dot(ext[...], jnp.concatenate([high, high, low], axis=0))

    code = rows_of(code_ref, d, 0, bag)
    weight = rows_of(vals_ref, d, 0, bag)
    cold = code - mine * cold_rows
    hot = code - all_rows - mine * hot_rows
    is_cold = (cold >= 0) & (cold < cold_rows) & (code < all_rows)
    is_hot = (hot >= 0) & (hot < hot_rows)
    owned = is_cold | is_hot
    row = jnp.where(is_cold, cold, hot + cold_rows) + 1
    ones = jnp.where(owned, 1.0, 0.0)
    rank = dot(earlier, ones.astype(BF16)).astype(I32)
    rank = jnp.where(owned, rank, -1)
    blocks = [slice(start, start + lanes) for start in range(0, examples, lanes)]
    owned_counts = jnp.sum(ones, axis=0, keepdims=True)
    counts = [jnp.max(owned_counts[:, here]).astype(I32) for here in blocks]
    most = functools.reduce(jnp.maximum, counts)

    def compact(i, _):
        for u in range(2):
            this = rank == 2 * i + u
            at = jnp.sum(jnp.where(this, row, 0), axis=0, keepdims=True) - 1
            w = jnp.sum(jnp.where(this, weight, 0.0), axis=0, keepdims=True)
            for c, here in enumerate(blocks):
                at_rank[c, pl.ds(2 * i + u, 1), :] = at[:, here]
                w_rank[c, pl.ds(2 * i + u, 1), :] = w[:, here]
        return 0

    lax.fori_loop(0, jnp.maximum((most + 1) // 2, 2), compact, 0)

    numbers = lax.broadcasted_iota(I32, (rows, lanes), 0)
    scores, squares = [], []
    for c, here in enumerate(blocks):

        def placed(start, number):
            total = 0.0
            for u in range(number):
                at = at_rank[c, pl.ds(start + u, 1), :]
                w = w_rank[c, pl.ds(start + u, 1), :]
                total = total + jnp.where(numbers == at, w, 0.0)
            return total

        acc[...] = placed(0, 4)

        def place(i, _):
            acc[...] += placed(2 * i, 2)
            return 0

        lax.fori_loop(2, (counts[c] + 1) // 2, place, 0)
        total = acc[...]
        high, low = split(total)
        high_ref[:, here] = high
        low_ref[:, here] = low
        scores.append(jnp.sum(total * shares[:, here], axis=0, keepdims=True))
        squares.append(jnp.sum(total * total, axis=0, keepdims=True))
    sums_ref[pl.ds(d, 1), :] = jnp.concatenate(scores, axis=1)
    sums_ref[pl.ds(data_count + d, 1), :] = jnp.concatenate(squares, axis=1)


def update_kernel(
    data_count, table_count, bag, sums_ref, vals_ref, high_hbm, low_hbm, cold_grad_ref, hot_grad_ref,
    high_ref, low_ref,
    over_table, over_data, hot_all, clip_all, load, as_, ar, bs, br, hs, hr, gs, gr,
):
    d = lax.axis_index("dp")
    t = lax.axis_index("table")
    loads = [
        pltpu.make_async_copy(high_hbm, high_ref, load.at[0]),
        pltpu.make_async_copy(low_hbm, low_ref, load.at[1]),
    ]
    data_peers = [(lax.rem(d + k, data_count), t) for k in range(1, data_count)]
    table_peers = [(d, lax.rem(t + k, table_count)) for k in range(1, table_count)]
    barrier = pltpu.get_barrier_semaphore()
    for peer in data_peers + table_peers:
        pl.semaphore_signal(barrier, inc=1, device_id=peer, device_id_type=MESH)
    for copy in loads:
        copy.start()
    pl.semaphore_wait(barrier, data_count + table_count - 2)

    def exchange(ref, at, peers, send_sem, recv_sem):
        return [
            remote(ref, at, peer, send_sem.at[k], recv_sem.at[k]) for k, peer in enumerate(peers)
        ]

    over_table[t] = sums_ref[...]
    for copy in exchange(over_table, t, table_peers, as_, ar):
        copy.wait()
    total = over_table[0]
    for k in range(1, table_count):
        total += over_table[k]
    over_data[d] = total
    for copy in exchange(over_data, d, data_peers, bs, br):
        copy.wait()
    total = over_data[0]
    for k in range(1, data_count):
        total += over_data[k]

    width, cold_rows = cold_grad_ref.shape
    examples = sums_ref.shape[1]
    rows = high_ref.shape[0]
    hot_rows = rows - cold_rows
    for k in range(data_count):
        items = rows_of(vals_ref, k, bag, bag + width)
        labels = tile_of(vals_ref, k, (bag + width) // 8)[0:1]
        residual = jax.nn.sigmoid(total[k : k + 1]) - labels
        grad = residual * items
        square = jnp.sum(grad * grad, axis=0, keepdims=True)
        norms = jnp.sqrt(total[data_count + k : data_count + k + 1] * square)
        high, low = split(grad * (CLIP_NORM / jnp.maximum(norms, CLIP_NORM)))
        here = pl.ds(k * examples, examples)
        clip_all[:width, here] = high
        clip_all[width:, here] = low

    for copy in loads:
        copy.wait()

    def gradient(start, size):
        both = dot_nt(clip_all[...], high_ref[pl.ds(start, size), :])
        rest = dot_nt(clip_all[:width, :], low_ref[pl.ds(start, size), :])
        return both[:width] + both[width:] + rest

    hot_own = gradient(cold_rows, hot_rows)
    mine = d * table_count + t
    half = width // 2
    hot_all[mine] = jnp.concatenate([hot_own[:half], hot_own[half:]], axis=1)
    first = exchange(hot_all, mine, data_peers, hs, hr)

    def update(start, size):
        here = pl.ds(start, size)
        cold_grad_ref[:, here] = gradient(start, size)

    step = cold_rows // 4
    update(0, step)
    for copy in first:
        copy.wait()
    second = []
    for k in range(data_count):
        at = lax.rem(d + k, data_count) * table_count + t
        second += exchange(hot_all, at, table_peers, gs.at[k], gr.at[k])
    for i in range(1, 4):
        update(i * step, step)
    for copy in second:
        copy.wait()
    for pair in range(data_count * table_count // 2):
        here = pl.ds(pair * 2 * hot_rows, 2 * hot_rows)
        left, right = hot_all[2 * pair], hot_all[2 * pair + 1]
        upper = jnp.concatenate([left[:, :hot_rows], right[:, :hot_rows]], axis=1)
        lower = jnp.concatenate([left[:, hot_rows:], right[:, hot_rows:]], axis=1)
        hot_grad_ref[:, here] = jnp.concatenate([upper, lower], axis=0)


def per_device(
    table_rows,
    hot_rows,
    bag_ids,
    bag_weights,
    items,
    labels,
    position_of,
    hot_ids,
    table_noise,
    hot_noise,
):
    cold_rows, width = table_rows.shape
    all_rows = position_of.shape[0]
    hot_count = hot_ids.shape[0]
    bag, examples = bag_ids.shape
    table_count = lax.axis_size("table")
    data_count = lax.axis_size("dp")
    devices = table_count * data_count
    mine = lax.axis_index("dp") * table_count + lax.axis_index("table")
    hot_own = hot_count // devices
    rows = cold_rows + hot_own
    high_count = all_rows // LOW
    planes = 1
    while 256**planes < all_rows + hot_count:
        planes += 1
    tiles = (bag + width) // 8 + 1
    chunk_rows = 8 * (-(-tiles // table_count))
    assert bag % 8 == 0 and bag // 8 <= table_count and 2 * hot_own == 128 and width == hot_own
    limit = 56 * 1024 * 1024
    vmem = pl.BlockSpec(memory_space=VMEM)
    dma = pltpu.SemaphoreType.DMA
    half = table_count // 2
    spread = [dma((data_count,))] * 2 + [dma((data_count, half))] * 4

    vals, code = pl.pallas_call(
        functools.partial(lookup_kernel, data_count, table_count, planes),
        out_shape=(
            jax.ShapeDtypeStruct((table_count, data_count, chunk_rows, examples), F32),
            jax.ShapeDtypeStruct((table_count, data_count, 8, examples), I32),
        ),
        in_specs=[vmem] * 6,
        out_specs=(vmem, vmem),
        scratch_shapes=[
            VMEM((high_count, LOW), F32),
            VMEM((planes * high_count, LOW), BF16),
        ]
        + spread
        + spread,
        compiler_params=pltpu.CompilerParams(
            collective_id=0, has_side_effects=True, vmem_limit_bytes=limit
        ),
    )(
        position_of.reshape(high_count, LOW),
        hot_ids.reshape(1, hot_count),
        bag_ids,
        bag_weights,
        items,
        labels.reshape(1, examples),
    )

    hot_mine = lax.dynamic_slice_in_dim(hot_rows, mine * hot_own, hot_own, 0)

    def whole(*shape):
        return pl.BlockSpec(shape, lambda d: (0,) * len(shape))

    high, low, sums = pl.pallas_call(
        functools.partial(weights_kernel, (data_count, table_count), bag, all_rows),
        grid=(data_count,),
        out_shape=(
            jax.ShapeDtypeStruct((rows, data_count * examples), BF16),
            jax.ShapeDtypeStruct((rows, data_count * examples), BF16),
            jax.ShapeDtypeStruct((2 * data_count, examples), F32),
        ),
        in_specs=[
            whole(*vals.shape),
            whole(*code.shape),
            whole(width, cold_rows),
            whole(width, hot_own),
        ],
        out_specs=(
            pl.BlockSpec((rows, examples), lambda d: (0, d)),
            pl.BlockSpec((rows, examples), lambda d: (0, d)),
            whole(2 * data_count, examples),
        ),
        scratch_shapes=[
            VMEM((rows, 128), F32),
            VMEM((rows, 3 * width), BF16),
            VMEM((rows, examples), F32),
            VMEM((examples // 128, bag, 128), I32),
            VMEM((examples // 128, bag, 128), F32),
        ],
        compiler_params=pltpu.CompilerParams(vmem_limit_bytes=limit),
    )(vals, code, table_rows.T, hot_mine.T)

    cold_grad, hot_grad = pl.pallas_call(
        functools.partial(update_kernel, data_count, table_count, bag),
        out_shape=(
            jax.ShapeDtypeStruct((width, cold_rows), F32),
            jax.ShapeDtypeStruct((width, hot_count), F32),
        ),
        in_specs=[vmem] * 2 + [pl.BlockSpec(memory_space=pl.ANY)] * 2,
        out_specs=(vmem, vmem),
        scratch_shapes=[
            VMEM((rows, data_count * examples), BF16),
            VMEM((rows, data_count * examples), BF16),
            VMEM((table_count, 2 * data_count, examples), F32),
            VMEM((data_count, 2 * data_count, examples), F32),
            VMEM((devices, width // 2, 2 * hot_own), F32),
            VMEM((2 * width, data_count * examples), BF16),
            dma((2,)),
            dma((table_count - 1,)),
            dma((table_count - 1,)),
            dma((data_count - 1,)),
            dma((data_count - 1,)),
            dma((data_count - 1,)),
            dma((data_count - 1,)),
            dma((data_count, table_count - 1)),
            dma((data_count, table_count - 1)),
        ],
        compiler_params=pltpu.CompilerParams(
            collective_id=1, has_side_effects=True, vmem_limit_bytes=limit
        ),
    )(sums, vals, high, low)
    new_table = table_rows - LEARN_RATE * (cold_grad.T + CLIP_NORM * table_noise)
    new_hot = hot_rows - LEARN_RATE * (hot_grad.T + CLIP_NORM * hot_noise)
    return (new_table, new_hot)


def solution(mesh):
    return jax.shard_map(
        per_device,
        mesh=mesh,
        in_specs=(
            P(("dp", "table"), None),
            P(),
            P(None, "dp"),
            P(None, "dp"),
            P(None, "dp"),
            P("dp"),
            P(),
            P(),
            P(("dp", "table"), None),
            P(),
        ),
        out_specs=(P(("dp", "table"), None), P()),
        check_vma=False,
    )
```

```python
import functools

import jax
import jax.numpy as jnp
from jax import lax
from jax.experimental import pallas as pl
from jax.experimental.pallas import tpu as pltpu
from jax.sharding import PartitionSpec as P

LEARN_RATE = 20.0
CLIP_NORM = 1.0
LOW = 128
MESH = pl.DeviceIdType.MESH
VMEM = pltpu.VMEM
F32, BF16, I32 = jnp.float32, jnp.bfloat16, jnp.int32
NT = (((1,), (1,)), ((), ()))


def dot(a, b):
    return jnp.dot(a, b, preferred_element_type=F32)


def dot_nt(a, b):
    return lax.dot_general(a, b, NT, preferred_element_type=F32)


def split(x):
    high = x.astype(BF16)
    return high, (x - high.astype(F32)).astype(BF16)


def remote(ref, at, peer, send_sem, recv_sem):
    copy = pltpu.make_async_remote_copy(
        src_ref=ref.at[at],
        dst_ref=ref.at[at],
        send_sem=send_sem,
        recv_sem=recv_sem,
        device_id=peer,
        device_id_type=MESH,
    )
    copy.start()
    return copy


class Spread:
    def __init__(self, ref, sizes, own, sems):
        self.ref, self.own, self.sems = ref, own, sems
        self.data_count, self.table_count = sizes
        self.d, self.t = lax.axis_index("dp"), lax.axis_index("table")
        self.alike = [
            lax.rem(self.t + 2 * i, self.table_count) for i in range(1, self.table_count // 2)
        ]
        self.partner = self.t + 1 - 2 * lax.rem(self.t, 2)
        self.first, self.second, self.third = [], [], []

    def group(self, k):
        return lax.rem(self.d + self.data_count - k, self.data_count)

    def over_data(self):
        for k in range(1, self.data_count):
            peer = (lax.rem(self.d + k, self.data_count), self.t)
            sems = self.sems[0].at[k], self.sems[1].at[k]
            self.first.append(remote(self.ref, (self.t, self.d), peer, *sems))

    def over_table(self):
        for k in range(0 if self.own else 1, self.data_count):
            if k:
                self.first[k - 1].wait_recv()
            at = (self.t, self.group(k))
            for i, peer in enumerate(self.alike):
                sems = self.sems[2].at[k, i], self.sems[3].at[k, i]
                self.second.append((k, i, remote(self.ref, at, (self.d, peer), *sems)))
            self.to_partner(k, 0)

    def to_partner(self, k, i):
        at = (lax.rem(self.t + self.table_count - 2 * i, self.table_count), self.group(k))
        sems = self.sems[4].at[k, i], self.sems[5].at[k, i]
        self.third.append(remote(self.ref, at, (self.d, self.partner), *sems))

    def over_pair(self):
        for k, i, copy in self.second:
            copy.wait_recv()
            self.to_partner(k, i + 1)

    def finish(self):
        for copy in self.third:
            copy.wait_recv()
        for copy in self.first + [copy for _, _, copy in self.second] + self.third:
            copy.wait_send()


def tile_of(ref, d, tile, lanes=slice(None)):
    per = ref.shape[2] // 8
    return ref[tile // per, d, tile % per * 8 : tile % per * 8 + 8, lanes]


def rows_of(ref, d, start, stop, lanes=slice(None)):
    return jnp.concatenate(
        [tile_of(ref, d, tile, lanes) for tile in range(start // 8, stop // 8)], axis=0
    )


def lookup_kernel(
    data_count, table_count, planes, pos_ref, hot_ref, ids_ref, w_ref, items_ref, lab_ref,
    vals_ref, code_ref, slots, table, *sems,
):
    d = lax.axis_index("dp")
    t = lax.axis_index("table")
    sizes = (data_count, table_count)
    vals = Spread(vals_ref, sizes, False, sems[:6])
    codes = Spread(code_ref, sizes, True, sems[6:])
    barrier = pltpu.get_barrier_semaphore()
    peers = [(lax.rem(d + k, data_count), t) for k in range(1, data_count)]
    peers += [(d, peer) for peer in vals.alike + [vals.partner]]
    for peer in peers:
        pl.semaphore_signal(barrier, inc=1, device_id=peer, device_id_type=MESH)
    bag, examples = w_ref.shape
    width = items_ref.shape[0]
    per = vals_ref.shape[2] // 8
    label = jnp.broadcast_to(lab_ref[...].astype(F32), (8, examples))
    for tile in range(table_count * per):
        start = tile * 8
        if start < bag:
            part = w_ref[start : start + 8, :]
        elif start < bag + width:
            part = items_ref[start - bag : start - bag + 8, :]
        else:
            part = label
        vals_ref[tile // per, d, tile % per * 8 : tile % per * 8 + 8, :] = part
    pl.semaphore_wait(barrier, len(peers))
    vals.over_data()

    high_count = pos_ref.shape[0]
    hot_count = hot_ref.shape[1]
    chunk = min(512, hot_count)
    slots[...] = jnp.zeros_like(slots)

    def add_hot(c, _):
        start = pl.multiple_of(c * chunk, chunk)
        hot = hot_ref[:, pl.ds(start, chunk)]
        number = start + 1 + lax.broadcasted_iota(I32, (1, chunk), 1)
        at_high = lax.broadcasted_iota(I32, (high_count, chunk), 0) == hot // LOW
        at_low = lax.broadcasted_iota(I32, (LOW, chunk), 0) == hot % LOW
        low_hot = jnp.where(at_low, 1.0, 0.0).astype(BF16)
        upper = jnp.where(at_high, (number // 256).astype(F32), 0.0).astype(BF16)
        lower = jnp.where(at_high, (number % 256).astype(F32), 0.0).astype(BF16)
        slots[...] += 256.0 * dot_nt(upper, low_hot) + dot_nt(lower, low_hot)
        return 0

    lax.fori_loop(0, hot_count // chunk, add_hot, 0)
    slot = slots[...].astype(I32)
    code = jnp.where(slot > 0, high_count * LOW - 1 + slot, pos_ref[...])
    for p in range(planes):
        part = lax.shift_right_logical(code, 8 * p) & 255
        table[p * high_count : (p + 1) * high_count, :] = part.astype(F32).astype(BF16)
    vals.over_table()

    mine = pl.multiple_of(jnp.minimum(t, bag // 8 - 1) * 8, 8)

    def look_up(j, _):
        ids = ids_ref[pl.ds(mine + j, 1), :]
        at_low = lax.broadcasted_iota(I32, (LOW, examples), 0) == ids % LOW
        found = dot(table[...], jnp.where(at_low, 1.0, 0.0).astype(BF16))
        at_high = lax.broadcasted_iota(I32, (high_count, examples), 0) == ids // LOW
        total = jnp.zeros((1, examples), F32)
        for p in range(planes):
            part = found[p * high_count : (p + 1) * high_count]
            total += (256.0**p) * jnp.sum(jnp.where(at_high, part, 0.0), axis=0, keepdims=True)
        code_ref[t, d, pl.ds(j, 1), :] = total.astype(I32)
        return 0

    lax.fori_loop(0, 8, look_up, 0)
    codes.over_data()
    codes.over_table()
    vals.over_pair()
    codes.over_pair()
    vals.finish()
    codes.finish()


def weights_kernel(
    sizes, bag, all_rows, vals_ref, code_ref, cold_ref, hot_ref, high_ref, low_ref, sums_ref,
    acc, ext, shares, at_rank, w_rank,
):
    data_count, table_count = sizes
    mine = lax.axis_index("dp") * table_count + lax.axis_index("table")
    d = pl.program_id(0)
    examples = code_ref.shape[3]
    width, cold_rows = cold_ref.shape
    hot_rows = hot_ref.shape[1] // (data_count * table_count)
    rows = cold_rows + hot_rows
    lanes = 128

    @pl.when(d == 0)
    def _():
        pair = pl.ds(pl.multiple_of(mine // 2 * (2 * hot_rows), 2 * hot_rows), 2 * hot_rows)
        two = hot_ref[:, pair].T
        hot_own = jnp.where(mine % 2 == 0, two[:hot_rows], two[hot_rows:])
        for start, part in ((0, cold_ref[...].T), (cold_rows, hot_own)):
            high, low = split(part)
            here = pl.ds(start, part.shape[0])
            ext[here, :width] = high
            ext[here, width : 2 * width] = low
            ext[here, 2 * width :] = high

    earlier = (
        lax.broadcasted_iota(I32, (bag, bag), 1) < lax.broadcasted_iota(I32, (bag, bag), 0)
    )
    earlier = jnp.where(earlier, 1.0, 0.0).astype(BF16)
    high, low = split(rows_of(vals_ref, d, bag, bag + width))
    shares[...] = dot(ext[...], jnp.concatenate([high, high, low], axis=0))

    code = rows_of(code_ref, d, 0, bag)
    weight = rows_of(vals_ref, d, 0, bag)
    cold = code - mine * cold_rows
    hot = code - all_rows - mine * hot_rows
    is_cold = (cold >= 0) & (cold < cold_rows) & (code < all_rows)
    is_hot = (hot >= 0) & (hot < hot_rows)
    owned = is_cold | is_hot
    row = jnp.where(is_cold, cold, hot + cold_rows) + 1
    ones = jnp.where(owned, 1.0, 0.0)
    rank = dot(earlier, ones.astype(BF16)).astype(I32)
    rank = jnp.where(owned, rank, -1)
    blocks = [slice(start, start + lanes) for start in range(0, examples, lanes)]
    owned_counts = jnp.sum(ones, axis=0, keepdims=True)
    counts = [jnp.max(owned_counts[:, here]).astype(I32) for here in blocks]
    most = functools.reduce(jnp.maximum, counts)

    def compact(i, _):
        for u in range(2):
            this = rank == 2 * i + u
            at = jnp.sum(jnp.where(this, row, 0), axis=0, keepdims=True) - 1
            w = jnp.sum(jnp.where(this, weight, 0.0), axis=0, keepdims=True)
            for c, here in enumerate(blocks):
                at_rank[c, pl.ds(2 * i + u, 1), :] = at[:, here]
                w_rank[c, pl.ds(2 * i + u, 1), :] = w[:, here]
        return 0

    lax.fori_loop(0, jnp.maximum((most + 1) // 2, 2), compact, 0)

    numbers = lax.broadcasted_iota(I32, (rows, lanes), 0)
    scores, squares = [], []
    for c, here in enumerate(blocks):

        def placed(start, number):
            total = 0.0
            for u in range(number):
                at = at_rank[c, pl.ds(start + u, 1), :]
                w = w_rank[c, pl.ds(start + u, 1), :]
                total = total + jnp.where(numbers == at, w, 0.0)
            return total

        acc[...] = placed(0, 4)

        def place(i, _):
            acc[...] += placed(2 * i, 2)
            return 0

        lax.fori_loop(2, (counts[c] + 1) // 2, place, 0)
        total = acc[...]
        high, low = split(total)
        high_ref[:, here] = high
        low_ref[:, here] = low
        scores.append(jnp.sum(total * shares[:, here], axis=0, keepdims=True))
        squares.append(jnp.sum(total * total, axis=0, keepdims=True))
    sums_ref[pl.ds(d, 1), :] = jnp.concatenate(scores, axis=1)
    sums_ref[pl.ds(data_count + d, 1), :] = jnp.concatenate(squares, axis=1)


def update_kernel(
    data_count, table_count, bag, sums_ref, vals_ref, high_hbm, low_hbm, cold_grad_ref, hot_grad_ref,
    high_ref, low_ref,
    over_table, over_data, hot_all, clip_all, load, as_, ar, bs, br, *hot_sems,
):
    d = lax.axis_index("dp")
    t = lax.axis_index("table")
    loads = [
        pltpu.make_async_copy(high_hbm, high_ref, load.at[0]),
        pltpu.make_async_copy(low_hbm, low_ref, load.at[1]),
    ]
    data_peers = [(lax.rem(d + k, data_count), t) for k in range(1, data_count)]
    table_peers = [(d, lax.rem(t + k, table_count)) for k in range(1, table_count)]
    barrier = pltpu.get_barrier_semaphore()
    for peer in data_peers + table_peers:
        pl.semaphore_signal(barrier, inc=1, device_id=peer, device_id_type=MESH)
    for copy in loads:
        copy.start()
    pl.semaphore_wait(barrier, data_count + table_count - 2)

    def exchange(ref, at, peers, send_sem, recv_sem):
        return [
            remote(ref, at, peer, send_sem.at[k], recv_sem.at[k]) for k, peer in enumerate(peers)
        ]

    over_table[t] = sums_ref[...]
    for copy in exchange(over_table, t, table_peers, as_, ar):
        copy.wait()
    total = over_table[0]
    for k in range(1, table_count):
        total += over_table[k]
    over_data[d] = total
    for copy in exchange(over_data, d, data_peers, bs, br):
        copy.wait()
    total = over_data[0]
    for k in range(1, data_count):
        total += over_data[k]

    width, cold_rows = cold_grad_ref.shape
    examples = sums_ref.shape[1]
    rows = high_ref.shape[0]
    hot_rows = rows - cold_rows
    for k in range(data_count):
        items = rows_of(vals_ref, k, bag, bag + width)
        labels = tile_of(vals_ref, k, (bag + width) // 8)[0:1]
        residual = jax.nn.sigmoid(total[k : k + 1]) - labels
        grad = residual * items
        square = jnp.sum(grad * grad, axis=0, keepdims=True)
        norms = jnp.sqrt(total[data_count + k : data_count + k + 1] * square)
        high, low = split(grad * (CLIP_NORM / jnp.maximum(norms, CLIP_NORM)))
        here = pl.ds(k * examples, examples)
        clip_all[:width, here] = high
        clip_all[width:, here] = low

    for copy in loads:
        copy.wait()

    def gradient(start, size):
        both = dot_nt(clip_all[...], high_ref[pl.ds(start, size), :])
        rest = dot_nt(clip_all[:width, :], low_ref[pl.ds(start, size), :])
        return both[:width] + both[width:] + rest

    hot_own = gradient(cold_rows, hot_rows)
    half = width // 2
    hot_all[t, d] = jnp.concatenate([hot_own[:half], hot_own[half:]], axis=1)
    hot = Spread(hot_all, (data_count, table_count), True, hot_sems)
    hot.over_data()

    def update(i):
        step = cold_rows // 4
        cold_grad_ref[:, pl.ds(i * step, step)] = gradient(i * step, step)

    update(0)
    hot.over_table()
    update(1)
    update(2)
    hot.over_pair()
    update(3)
    hot.finish()
    for pair in range(data_count * table_count // 2):
        here = pl.ds(pair * 2 * hot_rows, 2 * hot_rows)
        at = 2 * pair % table_count, 2 * pair // table_count
        left, right = hot_all[at[0], at[1]], hot_all[at[0] + 1, at[1]]
        upper = jnp.concatenate([left[:, :hot_rows], right[:, :hot_rows]], axis=1)
        lower = jnp.concatenate([left[:, hot_rows:], right[:, hot_rows:]], axis=1)
        hot_grad_ref[:, here] = jnp.concatenate([upper, lower], axis=0)


def per_device(
    table_rows,
    hot_rows,
    bag_ids,
    bag_weights,
    items,
    labels,
    position_of,
    hot_ids,
    table_noise,
    hot_noise,
):
    cold_rows, width = table_rows.shape
    all_rows = position_of.shape[0]
    hot_count = hot_ids.shape[0]
    bag, examples = bag_ids.shape
    table_count = lax.axis_size("table")
    data_count = lax.axis_size("dp")
    devices = table_count * data_count
    hot_own = hot_count // devices
    rows = cold_rows + hot_own
    high_count = all_rows // LOW
    planes = 1
    while 256**planes < all_rows + hot_count:
        planes += 1
    tiles = (bag + width) // 8 + 1
    chunk_rows = 8 * (-(-tiles // table_count))
    assert bag % 8 == 0 and bag // 8 <= table_count and 2 * hot_own == 128 and width == hot_own
    limit = 56 * 1024 * 1024
    vmem = pl.BlockSpec(memory_space=VMEM)
    dma = pltpu.SemaphoreType.DMA
    half = table_count // 2
    spread = [dma((data_count,))] * 2 + [dma((data_count, half))] * 4

    vals, code = pl.pallas_call(
        functools.partial(lookup_kernel, data_count, table_count, planes),
        out_shape=(
            jax.ShapeDtypeStruct((table_count, data_count, chunk_rows, examples), F32),
            jax.ShapeDtypeStruct((table_count, data_count, 8, examples), I32),
        ),
        in_specs=[vmem] * 6,
        out_specs=(vmem, vmem),
        scratch_shapes=[
            VMEM((high_count, LOW), F32),
            VMEM((planes * high_count, LOW), BF16),
        ]
        + spread
        + spread,
        compiler_params=pltpu.CompilerParams(
            collective_id=0, has_side_effects=True, vmem_limit_bytes=limit
        ),
    )(
        position_of.reshape(high_count, LOW),
        hot_ids.reshape(1, hot_count),
        bag_ids,
        bag_weights,
        items,
        labels.reshape(1, examples),
    )

    def whole(*shape):
        return pl.BlockSpec(shape, lambda d: (0,) * len(shape))

    high, low, sums = pl.pallas_call(
        functools.partial(weights_kernel, (data_count, table_count), bag, all_rows),
        grid=(data_count,),
        out_shape=(
            jax.ShapeDtypeStruct((rows, data_count * examples), BF16),
            jax.ShapeDtypeStruct((rows, data_count * examples), BF16),
            jax.ShapeDtypeStruct((2 * data_count, examples), F32),
        ),
        in_specs=[
            whole(*vals.shape),
            whole(*code.shape),
            whole(width, cold_rows),
            whole(width, hot_count),
        ],
        out_specs=(
            pl.BlockSpec((rows, examples), lambda d: (0, d)),
            pl.BlockSpec((rows, examples), lambda d: (0, d)),
            whole(2 * data_count, examples),
        ),
        scratch_shapes=[
            VMEM((rows, 128), F32),
            VMEM((rows, 3 * width), BF16),
            VMEM((rows, examples), F32),
            VMEM((examples // 128, bag, 128), I32),
            VMEM((examples // 128, bag, 128), F32),
        ],
        compiler_params=pltpu.CompilerParams(vmem_limit_bytes=limit),
    )(vals, code, table_rows.T, hot_rows.T)

    cold_grad, hot_grad = pl.pallas_call(
        functools.partial(update_kernel, data_count, table_count, bag),
        out_shape=(
            jax.ShapeDtypeStruct((width, cold_rows), F32),
            jax.ShapeDtypeStruct((width, hot_count), F32),
        ),
        in_specs=[vmem] * 2 + [pl.BlockSpec(memory_space=pl.ANY)] * 2,
        out_specs=(vmem, vmem),
        scratch_shapes=[
            VMEM((rows, data_count * examples), BF16),
            VMEM((rows, data_count * examples), BF16),
            VMEM((table_count, 2 * data_count, examples), F32),
            VMEM((data_count, 2 * data_count, examples), F32),
            VMEM((table_count, data_count, width // 2, 2 * hot_own), F32),
            VMEM((2 * width, data_count * examples), BF16),
            dma((2,)),
            dma((table_count - 1,)),
            dma((table_count - 1,)),
            dma((data_count - 1,)),
            dma((data_count - 1,)),
        ]
        + spread,
        compiler_params=pltpu.CompilerParams(
            collective_id=1, has_side_effects=True, vmem_limit_bytes=limit
        ),
    )(sums, vals, high, low)
    new_table = table_rows - LEARN_RATE * (cold_grad.T + CLIP_NORM * table_noise)
    new_hot = hot_rows - LEARN_RATE * (hot_grad.T + CLIP_NORM * hot_noise)
    return (new_table, new_hot)


def solution(mesh):
    return jax.shard_map(
        per_device,
        mesh=mesh,
        in_specs=(
            P(("dp", "table"), None),
            P(),
            P(None, "dp"),
            P(None, "dp"),
            P(None, "dp"),
            P("dp"),
            P(),
            P(),
            P(("dp", "table"), None),
            P(),
        ),
        out_specs=(P(("dp", "table"), None), P()),
        check_vma=False,
    )
```
